1024 devices in a mesh: blk: 32 (over z, core), col: 32 (over y, x).
Axes of the slice: x: 4, y: 8, z: 16, core: 2. Of those that a mesh axis runs over, the one named last changes fastest.
Arguments:
- three_center: bfloat16 [256, 128, 4, 128], P('blk'), may hold values from -6 to 6
- block_rows: int32 [256], P('blk'), may hold values from 0 to 31, as said below
- occupied: bfloat16 [4096, 4096], P('blk', 'col'), may hold values from -0.1875 to 0.1875
- virtual: bfloat16 [4096, 4096], P('blk'), may hold values from -0.5 to 0.5
Outputs:
- transformed: bfloat16 [4096, 16384], P('blk', 'col')
- response: float32 [4, 4], replicated
The draws below stay inside these ranges and needn't reach their ends.
Inputs may be any that keep to these rules, and one draw needn't show every extreme that they name: `block_rows`: the 8 entries of each index of blk are distinct.
All inputs are finite; a program needn't handle non-finite values.
Results may differ from the reference program's by a relative error of at most 0.0049.
Values may be sent and summed in bfloat16 or wider, within the bound.
A program may use at most 32 MiB of HBM per device.

```python
import math
import jax
import jax.numpy as jnp
from jax import lax

BS = 128
AUX = 4
NB_DEV = 8
NBASIS = 4096
N_BLK = 32


def draw_block_rows(key, part):
    key = jax.random.fold_in(key, 7)
    scores = jax.random.randint(key, (N_BLK, N_BLK), 0, 1 << 20) * N_BLK + jnp.arange(N_BLK)[None, :]
    chosen = jax.random.randint(jax.random.fold_in(key, 1), (), 0, N_BLK)
    column_ids = jnp.arange(N_BLK)[None, :]
    forced = (jnp.arange(N_BLK)[:, None] == chosen) & ((column_ids == 0) | (column_ids == N_BLK - 1))
    scores = jnp.where(forced, -1, scores)
    ordering = jnp.argsort(scores, axis=1)[:, :NB_DEV]
    return ordering.reshape(-1).astype(jnp.int32)


def steps_of(stream_key, extent, cuts, low, largest):
    factor_of, own = 1.0, jax.random.fold_in(stream_key, 6)
    for axis_at, shards_of in cuts:
        draws = jnp.exp(jax.random.uniform(jax.random.fold_in(own, axis_at), (shards_of,), jnp.float32, low / len(cuts), largest / len(cuts)))
        factor_of = factor_of * jnp.repeat(draws, extent[axis_at] // shards_of).reshape([-1 if axis == axis_at else 1 for axis in range(len(extent))])
    return factor_of


def scatter_about(rng, shape, spread, most, cuts=(), dtype=jnp.bfloat16):
    gain = steps_of(rng, shape, cuts, -0.22, 0.18) if cuts else 1.0
    values = jax.random.normal(rng, shape, jnp.float32) * spread * gain
    return jnp.minimum(jnp.maximum(values, -most), most).astype(dtype)


def setup_inputs(seed: int = 0) -> dict:
    splits = jax.random.split(jax.random.key(seed), 5)
    return {
        "three_center": scatter_about(splits[0], (N_BLK * NB_DEV, BS, AUX, BS), 1.0, 6.0, ((0, 32),)),
        "block_rows": draw_block_rows(jax.random.fold_in(splits[4], 71), 0),
        "occupied": scatter_about(splits[2], (NBASIS, NBASIS), (BS * NB_DEV) ** -0.5, 0.1875, ((0, 32), (1, 32))),
        "virtual": scatter_about(splits[3], (NBASIS, NBASIS), BS ** -0.5, 0.5, ((0, 32),)),
    }


def reference(three_center, block_rows, occupied, virtual):
    summed = jnp.zeros((NBASIS, NBASIS * AUX), jnp.float32)
    for owner in range(N_BLK):
        stacked = jnp.zeros((NBASIS, AUX * BS), jnp.float32)
        for index in range(NB_DEV):
            slot = owner * NB_DEV + index
            occ_rows = lax.dynamic_slice_in_dim(occupied, (block_rows[slot] * BS).astype(jnp.int32), BS, 0)
            stacked = stacked + jnp.dot(occ_rows.T, three_center[slot].reshape(BS, AUX * BS), preferred_element_type=jnp.float32)
        rounded = stacked.astype(jnp.bfloat16).reshape(NBASIS, AUX, BS).transpose(2, 0, 1).reshape(BS, NBASIS * AUX)
        virt_rows = virtual[owner * BS:(owner + 1) * BS]
        summed = summed + jnp.dot(virt_rows.T, rounded, preferred_element_type=jnp.float32)
    transformed = summed.astype(jnp.bfloat16)
    response = jnp.zeros((AUX, AUX), jnp.float32)
    for owner in range(N_BLK):
        for index in range(NB_DEV):
            slot = owner * NB_DEV + index
            start_col = (block_rows[slot] * BS * AUX).astype(jnp.int32)
            band = lax.dynamic_slice_in_dim(transformed[owner * BS:(owner + 1) * BS], start_col, BS * AUX, 1)
            tile = band.reshape(BS, BS, AUX).astype(jnp.float32)
            response = response + jnp.einsum('slp,lqs->pq', tile, three_center[slot].astype(jnp.float32))
    response = response / (BS * math.sqrt(N_BLK * NB_DEV))
    return (transformed, response)
```

```python
import functools
import math

import jax
import jax.numpy as jnp
from jax import lax
from jax.experimental import pallas as pl
from jax.experimental.pallas import tpu as pltpu
from jax.sharding import PartitionSpec as P

BS = 128
AUX = 4
CORES = 2
DIMS = (16, 8, 4)
MESH = pl.DeviceIdType.MESH


def kernel(
    dims, rows_ref, blocks_hbm, occ_hbm, virt_hbm, out_ref, resp_ref,
    occ_in, blocks_in, perm, blocks, chosen, occ_all, s_all, virt_all, acc, sum_z, sum_y, sum_x,
    in_sem, o_send, o_recv, op_send, op_recv, s_send, s_recv, sp_send, sp_recv,
    vz_send, vz_recv, vx_send, vx_recv, vy_send, vy_recv,
    rz_send, rz_recv, ry_send, ry_recv, rx_send, rx_recv,
):
    nz, ny, nx = dims
    nb = CORES * nz
    n_stored = blocks.shape[0] // BS
    share = BS // ny
    n_part = nb // nx
    half_z, half_y = nz // 2, ny // 2

    blk, col = lax.axis_index("blk"), lax.axis_index("col")
    z, core = lax.div(blk, CORES), lax.rem(blk, CORES)
    y, x = lax.div(col, nx), lax.rem(col, nx)

    def wrap(value, size):
        return lax.rem(value + 2 * size, size)

    def at_z(step, which=None):
        which = core if which is None else which
        return wrap(z + step, nz) * CORES + which

    right, left = (at_z(1), col), (at_z(-1), col)
    pair = (z * CORES + 1 - core, col)
    up, down = (blk, wrap(y + 1, ny) * nx + x), (blk, wrap(y - 1, ny) * nx + x)

    load_occ = pltpu.make_async_copy(occ_hbm, occ_in, in_sem.at[0])
    load_blocks = pltpu.make_async_copy(blocks_hbm, blocks_in, in_sem.at[1])
    load_occ.start()
    load_blocks.start()

    barrier = pltpu.get_barrier_semaphore()

    def greet(blk_to, col_to):
        pl.semaphore_signal(barrier, inc=1, device_id=(blk_to, col_to), device_id_type=MESH)

    @pl.loop(1, nb)
    def _(step):
        greet(wrap(blk + step, nb), col)

    @pl.loop(1, ny)
    def _(step):
        greet(blk, wrap(y + step, ny) * nx + x)

    @pl.loop(1, nx)
    def _(step):
        greet(z * CORES, y * nx + wrap(x + step, nx))
        greet(z * CORES + 1, y * nx + wrap(x + step, nx))

    load_occ.wait()
    occ_all[blk] = occ_in[...].T
    pl.semaphore_wait(barrier, (nb - 1) + (ny - 1) + CORES * (nx - 1))

    sent = []

    def send(src, dst, send_sem, recv_sem, to):
        copy = pltpu.make_async_remote_copy(
            src_ref=src, dst_ref=dst, send_sem=send_sem, recv_sem=recv_sem, device_id=to, device_id_type=MESH
        )
        copy.start()
        sent.append(copy)

    def arrive(ref, send_sem, recv_sem, source):
        pltpu.make_async_remote_copy(
            src_ref=ref, dst_ref=ref, send_sem=send_sem, recv_sem=recv_sem, device_id=source, device_id_type=MESH
        ).wait_recv()

    def occ_view(way, step, which=None):
        index = at_z(-step if way == 0 else step, which)
        return occ_all.at[index]

    def occ_half(way, which=None):
        index = at_z(half_z, which)
        return occ_all.at[index, pl.ds(way * (BS // 2), BS // 2)]

    def occ_forward(way, step):
        to = right if way == 0 else left
        if step + 1 < half_z:
            view = occ_view(way, step)
        else:
            index = at_z(-step if way == 0 else step)
            view = occ_all.at[index, pl.ds(way * (BS // 2), BS // 2)]
        send(view, view, o_send.at[way, step + 1], o_recv.at[way, step + 1], to)

    def occ_pair(way, step):
        view = occ_view(way, step) if step < half_z else occ_half(way)
        send(view, view, op_send.at[way, step], op_recv.at[way, step], pair)

    def occ_arrive(way, step):
        view = occ_view(way, step) if step < half_z else occ_half(way)
        arrive(view, o_send.at[way, step], o_recv.at[way, step], left if way == 0 else right)

    def occ_pair_arrive(way, step):
        view = occ_view(way, step, 1 - core) if step < half_z else occ_half(way, 1 - core)
        arrive(view, op_send.at[way, step], op_recv.at[way, step], pair)

    occ_forward(0, 0)
    occ_forward(1, 0)
    occ_pair(0, 0)

    def virt_part(part):
        return virt_all.at[y, x, part]

    def virt_source(to):
        return virt_hbm.at[pl.ds(y * share, share), pl.ds(pl.multiple_of(to * BS, BS), BS)]

    def virt_remote(part):
        to = wrap(blk + x + nx * part, nb)
        return pltpu.make_async_remote_copy(
            src_ref=virt_source(to), dst_ref=virt_part(part), send_sem=vz_send.at[part], recv_sem=vz_recv.at[part],
            device_id=(to, col), device_id_type=MESH,
        )

    def virt_local():
        return pltpu.make_async_copy(virt_source(blk), virt_part(0), vz_recv.at[0])

    @pl.when(x != 0)
    def _():
        virt_remote(0).start()

    @pl.when(x == 0)
    def _():
        virt_local().start()

    for part in range(1, n_part):
        virt_remote(part).start()

    row = lax.broadcasted_iota(jnp.int32, (AUX * BS, AUX * BS), 0)
    column = lax.broadcasted_iota(jnp.int32, (AUX * BS, AUX * BS), 1)
    perm[...] = (column == (row & (BS - 1)) * AUX + (row >> 7)).astype(jnp.float32).astype(jnp.bfloat16)
    load_blocks.wait()

    def order_blocks(index):
        rows = pl.ds(index * AUX * BS, AUX * BS)
        ordered = jnp.dot(perm[...], blocks_in[rows, :], preferred_element_type=jnp.float32).astype(jnp.bfloat16)
        for aux in range(AUX):
            blocks[pl.ds(index * BS, BS), pl.ds(aux * BS, BS)] = ordered[aux * BS:(aux + 1) * BS, :]

    def virt_arrived():
        @pl.when(x != 0)
        def _():
            virt_remote(0).wait()

        @pl.when(x == 0)
        def _():
            virt_local().wait()

        for part in range(1, n_part):
            virt_remote(part).wait()
        for step in range(1, nx):
            send(virt_all.at[y, x], virt_all.at[y, x], vx_send.at[step], vx_recv.at[step],
                 (blk, y * nx + wrap(x + step, nx)))

    def virt_y_send(way, step):
        to = up if way == 0 else down
        index = wrap(y - step if way == 0 else y + step, ny)
        if step + 1 < half_y:
            view = virt_all.at[index]
        else:
            view = virt_all.at[index, pl.ds(way * (nx // 2), nx // 2)]
        send(view, view, vy_send.at[way, step + 1], vy_recv.at[way, step + 1], to)

    def virt_y_arrive(way, step):
        index = wrap(y - step if way == 0 else y + step, ny)
        if step < half_y:
            view = virt_all.at[index]
        else:
            view = virt_all.at[index, pl.ds(way * (nx // 2), nx // 2)]
        arrive(view, vy_send.at[way, step], vy_recv.at[way, step], down if way == 0 else up)

    def virt_x_arrived():
        for step in range(1, nx):
            source = wrap(x - step, nx)
            arrive(virt_all.at[y, source], vx_send.at[step], vx_recv.at[step], (blk, y * nx + source))
        virt_y_send(0, 0)
        virt_y_send(1, 0)

    order_blocks(0)
    for step in range(1, half_z + 1):
        for way in (0, 1):
            occ_arrive(way, step)
            if step < half_z:
                occ_forward(way, step)
            occ_pair(way, step)
        if step < n_stored:
            order_blocks(step)
        if step == half_z // 2:
            virt_arrived()
    for index in range(half_z + 1, n_stored):
        order_blocks(index)
    virt_x_arrived()
    occ_pair_arrive(0, 0)
    for step in range(1, half_z + 1):
        for way in (0, 1):
            occ_pair_arrive(way, step)

    def s_view(way, step, sub, which=None):
        return s_all.at[at_z(-step if way == 0 else step, which), pl.ds(2 * sub, 2)]

    def s_forward(way, step, sub):
        if step + 1 < half_z or sub == way:
            view = s_view(way, step, sub)
            send(view, view, s_send.at[way, step + 1, sub], s_recv.at[way, step + 1, sub], right if way == 0 else left)

    def s_pair(way, step, sub):
        view = s_view(way, step, sub)
        send(view, view, sp_send.at[way, step, sub], sp_recv.at[way, step, sub], pair)

    def s_arrive(way, step, sub):
        arrive(s_view(way, step, sub), s_send.at[way, step, sub], s_recv.at[way, step, sub],
               left if way == 0 else right)

    def s_pair_arrive(way, step, sub):
        arrive(s_view(way, step, sub, 1 - core), sp_send.at[way, step, sub], sp_recv.at[way, step, sub], pair)

    occ_rows = jnp.concatenate([occ_all[rows_ref[index]] for index in range(n_stored)], axis=1)
    for sub in (0, 1):
        sums = jnp.dot(
            occ_rows, blocks[:, sub * 2 * BS:(sub + 1) * 2 * BS], preferred_element_type=jnp.float32
        ).astype(jnp.bfloat16)
        for aux in (0, 1):
            s_all[blk, 2 * sub + aux] = sums[:, aux * BS:(aux + 1) * BS]
        s_forward(0, 0, sub)
        s_forward(1, 0, sub)
        s_pair(0, 0, sub)

    picked = jnp.zeros((BS, AUX * BS), jnp.float32)
    for index in range(n_stored):
        here = (rows_ref[index] == col).astype(jnp.float32)
        picked = picked + blocks[index * BS:(index + 1) * BS, :].astype(jnp.float32) * here
    chosen[...] = picked

    def contribute(way, step, sub, first=False):
        base = wrap(z - step if way == 0 else z + step, nz)
        pieces, rows = [], []
        for which in range(CORES):
            index = base * CORES + which
            pieces.append(s_all[index, 2 * sub:2 * sub + 2].reshape(2 * BS, BS))
            away = wrap(blk - index, nb)
            rows.append(virt_all[:, lax.rem(away, nx), lax.div(away, nx)].reshape(BS, BS))
        term = jnp.dot(
            jnp.concatenate(pieces, axis=1), jnp.concatenate(rows, axis=0), preferred_element_type=jnp.float32
        )
        where = pl.ds(sub * 2 * BS, 2 * BS)
        acc[where, :] = term if first else acc[where, :] + term

    def contribute_step(step):
        if step == 0:
            for sub in (0, 1):
                s_pair_arrive(0, 0, sub)
                contribute(0, 0, sub, first=True)
        else:
            for sub in (0, 1):
                for way in (0, 1):
                    if step < half_z or sub == way:
                        s_pair_arrive(way, step, sub)
                        contribute(way, step, sub)

    done = 0
    for step in range(1, half_z + 1):
        for sub in (0, 1):
            for way in (0, 1):
                if step < half_z or sub == way:
                    s_arrive(way, step, sub)
                    if step < half_z:
                        s_forward(way, step, sub)
                    s_pair(way, step, sub)
        if step <= half_y:
            for way in (0, 1):
                virt_y_arrive(way, step)
                if step < half_y:
                    virt_y_send(way, step)
        if step >= half_y:
            for _ in range(2):
                if done < step:
                    contribute_step(done)
                    done += 1
    while done <= half_z:
        contribute_step(done)
        done += 1

    rounded = acc[...].astype(jnp.bfloat16)
    tiles = rounded.astype(jnp.float32)
    lane = lax.broadcasted_iota(jnp.int32, (1, BS), 1)
    message = jnp.zeros((1, BS), jnp.float32)
    for first in range(AUX):
        tile = tiles[first * BS:(first + 1) * BS, :]
        for second in range(AUX):
            product = tile * chosen[:, second * BS:(second + 1) * BS]
            total = jnp.sum(jnp.sum(product, axis=0, keepdims=True), axis=1, keepdims=True)
            message = message + jnp.where(lane == first * AUX + second, total, 0.0)

    def exchange(buffer, mine, members, send_sem, recv_sem, device_of, value):
        buffer[mine] = value

        def copy_to(step, slot):
            return pltpu.make_async_remote_copy(
                src_ref=buffer.at[slot], dst_ref=buffer.at[slot], send_sem=send_sem.at[step],
                recv_sem=recv_sem.at[slot], device_id=device_of(wrap(mine + step, members)), device_id_type=MESH,
            )

        @pl.loop(1, members)
        def _(step):
            copy_to(step, mine).start()

        def collect():
            @pl.loop(1, members)
            def _(step):
                copy_to(step, wrap(mine + step, members)).wait_recv()

            @pl.loop(1, members)
            def _(step):
                copy_to(step, mine).wait_send()

            return jnp.sum(buffer[...], axis=0)

        return collect

    collect = exchange(sum_z, z, nz, rz_send, rz_recv, lambda to: (to * CORES + core, col), message)
    out_ref[...] = lax.dot_general(
        rounded, perm[...], (((0,), (0,)), ((), ())), preferred_element_type=jnp.float32
    ).astype(jnp.bfloat16)
    message = collect()
    message = exchange(sum_y, y, ny, ry_send, ry_recv, lambda to: (blk, to * nx + x), message)()
    message = exchange(
        sum_x, core * nx + x, CORES * nx, rx_send, rx_recv,
        lambda to: (z * CORES + lax.div(to, nx), y * nx + lax.rem(to, nx)), message,
    )()

    scale = 1.0 / (BS * math.sqrt(nb * n_stored))
    value = jnp.broadcast_to(message, (AUX, BS)) * scale
    lanes = lax.broadcasted_iota(jnp.int32, (AUX, BS), 1)
    firsts = lax.broadcasted_iota(jnp.int32, (AUX, BS), 0)
    place = lax.broadcasted_iota(jnp.int32, (AUX, AUX), 1)
    response = jnp.zeros((AUX, AUX), jnp.float32)
    for second in range(AUX):
        picked = jnp.sum(jnp.where(lanes == firsts * AUX + second, value, 0.0), axis=1, keepdims=True)
        response = response + jnp.where(place == second, picked, 0.0)
    resp_ref[...] = response

    for copy in sent:
        copy.wait_send()


def per_device(dims, three_center, block_rows, occupied, virtual):
    nz, ny, nx = dims
    nb = CORES * nz
    n_stored = three_center.shape[0]
    half_z, half_y = nz // 2, ny // 2
    any_space = pl.BlockSpec(memory_space=pl.ANY)
    vmem = pl.BlockSpec(memory_space=pltpu.VMEM)
    bf16, f32 = jnp.bfloat16, jnp.float32
    dma = pltpu.SemaphoreType.DMA
    return pl.pallas_call(
        functools.partial(kernel, dims),
        out_shape=(
            jax.ShapeDtypeStruct((BS, AUX * BS), bf16),
            jax.ShapeDtypeStruct((AUX, AUX), f32),
        ),
        in_specs=[pl.BlockSpec(memory_space=pltpu.SMEM), any_space, any_space, any_space],
        out_specs=(vmem, vmem),
        scratch_shapes=[
            pltpu.VMEM((BS, BS), bf16),
            pltpu.VMEM((n_stored * BS * AUX, BS), bf16),
            pltpu.VMEM((AUX * BS, AUX * BS), bf16),
            pltpu.VMEM((n_stored * BS, AUX * BS), bf16),
            pltpu.VMEM((BS, AUX * BS), f32),
            pltpu.VMEM((nb, BS, BS), bf16),
            pltpu.VMEM((nb, AUX, BS, BS), bf16),
            pltpu.VMEM((ny, nx, nb // nx, BS // ny, BS), bf16),
            pltpu.VMEM((AUX * BS, BS), f32),
            pltpu.VMEM((nz, 1, BS), f32),
            pltpu.VMEM((ny, 1, BS), f32),
            pltpu.VMEM((CORES * nx, 1, BS), f32),
            dma((2,)),
            dma((2, half_z + 1)), dma((2, half_z + 1)),
            dma((2, half_z + 1)), dma((2, half_z + 1)),
            dma((2, half_z + 1, 2)), dma((2, half_z + 1, 2)),
            dma((2, half_z + 1, 2)), dma((2, half_z + 1, 2)),
            dma((nb // nx,)), dma((nb // nx,)),
            dma((nx,)), dma((nx,)),
            dma((2, half_y + 1)), dma((2, half_y + 1)),
            dma((nz,)), dma((nz,)),
            dma((ny,)), dma((ny,)),
            dma((CORES * nx,)), dma((CORES * nx,)),
        ],
        compiler_params=pltpu.CompilerParams(
            collective_id=0, has_side_effects=True, vmem_limit_bytes=32 * 1024 * 1024
        ),
    )(block_rows, three_center.reshape(-1, BS), occupied, virtual)


def solution(mesh):
    in_specs = (P("blk", None, None, None), P("blk"), P("blk", "col"), P("blk", None))
    out_specs = (P("blk", "col"), P())
    return jax.shard_map(
        functools.partial(per_device, DIMS), mesh=mesh, in_specs=in_specs, out_specs=out_specs, check_vma=False
    )
```

```python
import functools
import math

import jax
import jax.numpy as jnp
from jax import lax
from jax.experimental import pallas as pl
from jax.experimental.pallas import tpu as pltpu
from jax.sharding import PartitionSpec as P

BS = 128
AUX = 4
CORES = 2
DIMS = (16, 8, 4)
MESH = pl.DeviceIdType.MESH
V_STEP = 2
OCC_FROM = {1: 0, 2: 0, 3: 0, 4: 3, 5: 3, 6: 3, 7: 6, 8: 6}


def kernel(
    dims, rows_ref, blocks_hbm, occ_hbm, virt_hbm, out_ref, resp_ref,
    occ_in, blocks_in, wide, blocks, chosen, occ_all, s_all, virt_all, acc, spread, sum_z, sum_c,
    in_sem, o_send, o_recv, op_send, op_recv, s_send, s_recv, sp_send, sp_recv,
    vz_send, vz_recv, vx_send, vx_recv, vy_send, vy_recv, r_send, r_recv,
):
    nz, ny, nx = dims
    nb = CORES * nz
    n_stored = blocks.shape[0] // BS
    share = BS // ny
    n_part = nb // nx
    half_z, half_y = nz // 2, ny // 2

    blk, col = lax.axis_index("blk"), lax.axis_index("col")
    z, core = lax.div(blk, CORES), lax.rem(blk, CORES)
    y, x = lax.div(col, nx), lax.rem(col, nx)

    def wrap(value, size):
        return lax.rem(value + 2 * size, size)

    def at_z(step, which=None):
        which = core if which is None else which
        return wrap(z + step, nz) * CORES + which

    right, left = (at_z(1), col), (at_z(-1), col)
    pair = (z * CORES + 1 - core, col)
    up, down = (blk, wrap(y + 1, ny) * nx + x), (blk, wrap(y - 1, ny) * nx + x)

    load_occ = pltpu.make_async_copy(occ_hbm, occ_in, in_sem.at[0])
    load_blocks = pltpu.make_async_copy(blocks_hbm, blocks_in, in_sem.at[1])
    load_occ.start()
    load_blocks.start()

    barrier = pltpu.get_barrier_semaphore()
    near_z = [hops for hops in sorted({reach - start for reach, start in OCC_FROM.items()}) if hops <= half_z]
    greeted = [(at_z(sign * hops), col) for hops in near_z for sign in (1, -1)] + [pair, up, down]
    greeted += [(blk, y * nx + wrap(x + step, nx)) for step in range(1, nx)]
    for device in greeted:
        pl.semaphore_signal(barrier, inc=1, device_id=device, device_id_type=MESH)
    load_occ.wait()
    occ_all[blk] = occ_in[...].T
    pl.semaphore_wait(barrier, len(greeted))

    def send(src, dst, send_sem, recv_sem, to):
        copy = pltpu.make_async_remote_copy(
            src_ref=src, dst_ref=dst, send_sem=send_sem, recv_sem=recv_sem, device_id=to, device_id_type=MESH
        )
        copy.start()

    def arrive(ref, send_sem, recv_sem, source):
        pltpu.make_async_remote_copy(
            src_ref=ref, dst_ref=ref, send_sem=send_sem, recv_sem=recv_sem, device_id=source, device_id_type=MESH
        ).wait_recv()

    def occ_view(way, step, part, which=None):
        index = at_z(-step if way == 0 else step, which)
        if part < half_z:
            return occ_all.at[index]
        return occ_all.at[index, pl.ds(way * (BS // 2), BS // 2)]

    def occ_forward(way, step):
        for reach in range(half_z, step, -1):
            if OCC_FROM[reach] == step:
                view = occ_view(way, step, reach)
                hops = reach - step
                send(view, view, o_send.at[0], o_recv.at[way, reach], (at_z(hops if way == 0 else -hops), col))

    def occ_pair(way, step):
        view = occ_view(way, step, step)
        send(view, view, op_send.at[0], op_recv.at[way, step], pair)

    def occ_arrive(way, step):
        hops = step - OCC_FROM[step]
        arrive(occ_view(way, step, step), o_send.at[0], o_recv.at[way, step],
               (at_z(-hops if way == 0 else hops), col))

    def occ_pair_arrive(way, step):
        arrive(occ_view(way, step, step, 1 - core), op_send.at[0], op_recv.at[way, step], pair)

    occ_forward(0, 0)
    occ_forward(1, 0)
    occ_pair(0, 0)

    def virt_part(part):
        return virt_all.at[y, x, part]

    def virt_source(to):
        return virt_hbm.at[pl.ds(y * share, share), pl.ds(pl.multiple_of(to * BS, BS), BS)]

    def virt_remote(part):
        to = wrap(blk + x + nx * part, nb)
        return pltpu.make_async_remote_copy(
            src_ref=virt_source(to), dst_ref=virt_part(part), send_sem=vz_send.at[part], recv_sem=vz_recv.at[part],
            device_id=(to, col), device_id_type=MESH,
        )

    def virt_local():
        return pltpu.make_async_copy(virt_source(blk), virt_part(0), vz_recv.at[0])

    def virt_start():
        @pl.when(x != 0)
        def _():
            virt_remote(0).start()

        @pl.when(x == 0)
        def _():
            virt_local().start()

        for part in range(1, n_part):
            virt_remote(part).start()

    load_blocks.wait()

    def order_blocks(index):
        base = index * AUX * BS
        wide[pl.ds(base, AUX * BS), :] = blocks_in[pl.ds(base, AUX * BS), :].astype(jnp.float32)
        for aux in range(AUX):
            blocks[pl.ds(index * BS, BS), pl.ds(aux * BS, BS)] = wide[pl.ds(base + aux, BS, stride=AUX), :].astype(
                jnp.bfloat16
            )

    def virt_arrived():
        @pl.when(x != 0)
        def _():
            virt_remote(0).wait()

        @pl.when(x == 0)
        def _():
            virt_local().wait()

        for part in range(1, n_part):
            virt_remote(part).wait()
        for step in range(1, nx):
            send(virt_all.at[y, x], virt_all.at[y, x], vx_send.at[0], vx_recv.at[step],
                 (blk, y * nx + wrap(x + step, nx)))

    def virt_y_view(way, step, sub):
        return virt_all.at[wrap(y - step if way == 0 else y + step, ny), pl.ds(sub * (nx // 2), nx // 2)]

    def virt_y_send(way, step, sub):
        if step + 1 < half_y or sub == way:
            view = virt_y_view(way, step, sub)
            send(view, view, vy_send.at[0], vy_recv.at[way, step + 1, sub], up if way == 0 else down)

    def virt_y_step(step):
        for sub in (0, 1):
            for way in (0, 1):
                if step < half_y or sub == way:
                    arrive(virt_y_view(way, step, sub), vy_send.at[0], vy_recv.at[way, step, sub],
                           down if way == 0 else up)
                    if step < half_y:
                        virt_y_send(way, step, sub)

    def virt_x_arrived():
        for step in range(1, nx):
            source = wrap(x - step, nx)
            arrive(virt_all.at[y, source], vx_send.at[0], vx_recv.at[step], (blk, y * nx + source))
        for sub in (0, 1):
            virt_y_send(0, 0, sub)
            virt_y_send(1, 0, sub)

    for index in range(n_stored):
        order_blocks(index)
    for step in range(1, half_z + 1):
        for way in (0, 1):
            occ_arrive(way, step)
            if step < half_z:
                occ_forward(way, step)
        for way in (0, 1):
            occ_pair(way, step)
    occ_pair_arrive(0, 0)
    for step in range(1, half_z + 1):
        for way in (0, 1):
            occ_pair_arrive(way, step)

    def s_view(way, step, sub, which=None):
        return s_all.at[at_z(-step if way == 0 else step, which), sub]

    def s_forward(way, step, sub):
        if step + 1 < half_z or sub // 2 == way:
            view = s_view(way, step, sub)
            send(view, view, s_send.at[0], s_recv.at[way, step + 1, sub], right if way == 0 else left)

    def s_pair(way, step, sub):
        view = s_view(way, step, sub)
        send(view, view, sp_send.at[0], sp_recv.at[way, step, sub], pair)

    def s_arrive(way, step, sub):
        arrive(s_view(way, step, sub), s_send.at[0], s_recv.at[way, step, sub],
               left if way == 0 else right)

    def s_pair_arrive(way, step, sub):
        arrive(s_view(way, step, sub, 1 - core), sp_send.at[0], sp_recv.at[way, step, sub], pair)

    occ_rows = jnp.concatenate([occ_all[rows_ref[index]] for index in range(n_stored)], axis=1)
    for half in (0, 1):
        sums = jnp.dot(
            occ_rows, blocks[:, half * 2 * BS:(half + 1) * 2 * BS], preferred_element_type=jnp.float32
        ).astype(jnp.bfloat16)
        for sub in (2 * half, 2 * half + 1):
            s_all[blk, sub] = sums[:, (sub % 2) * BS:(sub % 2 + 1) * BS]
            s_forward(0, 0, sub)
            s_forward(1, 0, sub)
        for sub in (2 * half, 2 * half + 1):
            s_pair(0, 0, sub)
    virt_start()

    picked = jnp.zeros((BS, AUX * BS), jnp.float32)
    for index in range(n_stored):
        here = (rows_ref[index] == col).astype(jnp.float32)
        picked = picked + blocks[index * BS:(index + 1) * BS, :].astype(jnp.float32) * here
    chosen[...] = picked

    def contribute(way, step, half, first=False):
        base = wrap(z - step if way == 0 else z + step, nz)
        pieces, rows = [], []
        for which in range(CORES):
            index = base * CORES + which
            pieces.append(s_all[index, 2 * half:2 * half + 2].reshape(2 * BS, BS))
            away = wrap(blk - index, nb)
            rows.append(virt_all[:, lax.rem(away, nx), lax.div(away, nx)].reshape(BS, BS))
        term = jnp.dot(
            jnp.concatenate(pieces, axis=1), jnp.concatenate(rows, axis=0), preferred_element_type=jnp.float32
        )
        where = pl.ds(half * 2 * BS, 2 * BS)
        acc[where, :] = term if first else acc[where, :] + term

    def contribute_step(step):
        for half in (0, 1):
            for way in (0, 1):
                if (step < half_z or half == way) and (step > 0 or way == 0):
                    s_pair_arrive(way, step, 2 * half)
                    s_pair_arrive(way, step, 2 * half + 1)
                    contribute(way, step, half, first=step == 0)

    virt_steps = [virt_arrived, virt_x_arrived]
    virt_steps += [functools.partial(virt_y_step, step) for step in range(1, half_y + 1)]
    done = 0
    for step in range(1, half_z + 1):
        for sub in range(AUX):
            ways = [way for way in (0, 1) if step < half_z or sub // 2 == way]
            for way in ways:
                s_arrive(way, step, sub)
                if step < half_z:
                    s_forward(way, step, sub)
            for way in ways:
                s_pair(way, step, sub)
        if step >= V_STEP and virt_steps:
            virt_steps.pop(0)()
    for virt_step in virt_steps:
        virt_step()
    while done <= half_z:
        contribute_step(done)
        done += 1

    tiles = acc[...].astype(jnp.bfloat16).astype(jnp.float32)
    sums = []
    for first in range(AUX):
        tile = tiles[first * BS:(first + 1) * BS, :]
        for second in range(AUX):
            sums.append(jnp.sum(tile * chosen[:, second * BS:(second + 1) * BS], axis=0, keepdims=True))
    total = jnp.sum(jnp.concatenate(sums, axis=0), axis=1, keepdims=True)
    pairs = lax.broadcasted_iota(jnp.int32, (AUX * AUX, BS), 0)
    lanes = lax.broadcasted_iota(jnp.int32, (AUX * AUX, BS), 1)
    message = jnp.sum(jnp.where(pairs == lanes, total, 0.0), axis=0, keepdims=True)

    def exchange(buffer, mine, members, stage, device_of, value):
        buffer[mine] = value

        def copy_to(slot, to):
            return pltpu.make_async_remote_copy(
                src_ref=buffer.at[slot], dst_ref=buffer.at[slot], send_sem=r_send.at[stage],
                recv_sem=r_recv.at[stage], device_id=device_of(to), device_id_type=MESH,
            )

        @pl.loop(0, members - 1)
        def _(turn):
            away = lax.div(turn + 1, 2)
            step = members // 2 + away * (1 - 2 * lax.rem(turn, 2))
            copy_to(mine, wrap(mine + step, members)).start()

        def everything():
            some = buffer.at[pl.ds(0, members - 1)]
            return pltpu.make_async_remote_copy(
                src_ref=some, dst_ref=some, send_sem=r_send.at[stage], recv_sem=r_recv.at[stage],
                device_id=device_of(mine), device_id_type=MESH,
            )

        return everything

    over_z = exchange(sum_z, blk, nb, 0, lambda to: (to, col), message)

    for aux in range(AUX):
        spread[pl.ds(aux, BS, stride=AUX), :] = tiles[aux * BS:(aux + 1) * BS, :]
    out_ref[...] = spread[...].T.astype(jnp.bfloat16)

    def all_sent(ref, sem):
        pltpu.make_async_remote_copy(
            src_ref=ref, dst_ref=ref, send_sem=sem.at[0], recv_sem=o_recv.at[0, 0], device_id=pair, device_id_type=MESH
        ).wait_send()

    all_sent(occ_all.at[pl.ds(0, nz - 1)], o_send)
    all_sent(occ_all.at[pl.ds(0, nz)], op_send)
    all_sent(s_all.at[pl.ds(0, nz - 1)], s_send)
    all_sent(s_all.at[pl.ds(0, nz)], sp_send)
    all_sent(virt_all.at[0, pl.ds(0, nx - 1)], vx_send)
    all_sent(virt_all.at[pl.ds(0, ny - 1)], vy_send)

    over_z().wait_recv()
    message = jnp.sum(sum_z[...], axis=0)
    over_col = exchange(sum_c, col, ny * nx, 1, lambda to: (blk, to), message)
    over_z().wait_send()
    over_col().wait_recv()
    message = jnp.sum(sum_c[...], axis=0)

    scale = 1.0 / (BS * math.sqrt(nb * n_stored))
    value = jnp.broadcast_to(message, (AUX, BS)) * scale
    lanes = lax.broadcasted_iota(jnp.int32, (AUX, BS), 1)
    firsts = lax.broadcasted_iota(jnp.int32, (AUX, BS), 0)
    place = lax.broadcasted_iota(jnp.int32, (AUX, AUX), 1)
    response = jnp.zeros((AUX, AUX), jnp.float32)
    for second in range(AUX):
        picked = jnp.sum(jnp.where(lanes == firsts * AUX + second, value, 0.0), axis=1, keepdims=True)
        response = response + jnp.where(place == second, picked, 0.0)
    resp_ref[...] = response
    over_col().wait_send()


def per_device(dims, three_center, block_rows, occupied, virtual):
    nz, ny, nx = dims
    nb = CORES * nz
    n_stored = three_center.shape[0]
    half_z, half_y = nz // 2, ny // 2
    any_space = pl.BlockSpec(memory_space=pl.ANY)
    vmem = pl.BlockSpec(memory_space=pltpu.VMEM)
    bf16, f32 = jnp.bfloat16, jnp.float32
    dma = pltpu.SemaphoreType.DMA
    return pl.pallas_call(
        functools.partial(kernel, dims),
        out_shape=(
            jax.ShapeDtypeStruct((BS, AUX * BS), bf16),
            jax.ShapeDtypeStruct((AUX, AUX), f32),
        ),
        in_specs=[pl.BlockSpec(memory_space=pltpu.SMEM), any_space, any_space, any_space],
        out_specs=(vmem, vmem),
        scratch_shapes=[
            pltpu.VMEM((BS, BS), bf16),
            pltpu.VMEM((n_stored * BS * AUX, BS), bf16),
            pltpu.VMEM((n_stored * BS * AUX, BS), f32),
            pltpu.VMEM((n_stored * BS, AUX * BS), bf16),
            pltpu.VMEM((BS, AUX * BS), f32),
            pltpu.VMEM((nb, BS, BS), bf16),
            pltpu.VMEM((nb, AUX, BS, BS), bf16),
            pltpu.VMEM((ny, nx, nb // nx, BS // ny, BS), bf16),
            pltpu.VMEM((AUX * BS, BS), f32),
            pltpu.VMEM((AUX * BS, BS), f32),
            pltpu.VMEM((nb, 1, BS), f32),
            pltpu.VMEM((ny * nx, 1, BS), f32),
            dma((2,)),
            dma((1,)), dma((2, half_z + 1)),
            dma((1,)), dma((2, half_z + 1)),
            dma((1,)), dma((2, half_z + 1, AUX)),
            dma((1,)), dma((2, half_z + 1, AUX)),
            dma((nb // nx,)), dma((nb // nx,)),
            dma((1,)), dma((nx,)),
            dma((1,)), dma((2, half_y + 1, 2)),
            dma((2,)), dma((2,)),
        ],
        compiler_params=pltpu.CompilerParams(
            collective_id=0, has_side_effects=True, vmem_limit_bytes=60 * 1024 * 1024
        ),
    )(block_rows, three_center.reshape(-1, BS), occupied, virtual)


def solution(mesh):
    in_specs = (P("blk", None, None, None), P("blk"), P("blk", "col"), P("blk", None))
    out_specs = (P("blk", "col"), P())
    return jax.shard_map(
        functools.partial(per_device, DIMS), mesh=mesh, in_specs=in_specs, out_specs=out_specs, check_vma=False
    )
```

```python
import functools
import math

import jax
import jax.numpy as jnp
from jax import lax
from jax.experimental import pallas as pl
from jax.experimental.pallas import tpu as pltpu
from jax.sharding import PartitionSpec as P

BS = 128
AUX = 4
CORES = 2
DIMS = (16, 8, 4)
MESH = pl.DeviceIdType.MESH
VIRT_AT = (1, 3, 5, 6)
OCC_FROM = {1: 0, 2: 0, 3: 0, 4: 3, 5: 3, 6: 3, 7: 6, 8: 6}


def kernel(
    dims, rows_ref, blocks_hbm, occ_hbm, virt_hbm, out_ref, resp_ref,
    occ_in, blocks_in, wide, blocks, chosen, occ_low, occ_high, s_all, virt_all, acc, spread, sum_z, sum_c,
    in_sem, o_send, o_recv, op_send, op_recv, s_send, s_recv, sp_send, sp_recv, so_recv,
    vz_send, vz_recv, vx_send, vx_recv, vy_send, vy_recv, r_send, r_recv,
):
    nz, ny, nx = dims
    nb = CORES * nz
    n_stored = blocks.shape[0] // BS
    share = BS // ny
    n_part = nb // nx
    half_z, half_y = nz // 2, ny // 2

    blk, col = lax.axis_index("blk"), lax.axis_index("col")
    z, core = lax.div(blk, CORES), lax.rem(blk, CORES)
    y, x = lax.div(col, nx), lax.rem(col, nx)

    def wrap(value, size):
        return lax.rem(value + 2 * size, size)

    def at_z(step, which=None):
        which = core if which is None else which
        return wrap(z + step, nz) * CORES + which

    right, left = (at_z(1), col), (at_z(-1), col)
    pair = (z * CORES + 1 - core, col)
    up, down = (blk, wrap(y + 1, ny) * nx + x), (blk, wrap(y - 1, ny) * nx + x)

    load_occ = pltpu.make_async_copy(occ_hbm, occ_in, in_sem.at[0])
    load_blocks = pltpu.make_async_copy(blocks_hbm, blocks_in, in_sem.at[1])
    load_occ.start()
    load_blocks.start()

    barrier = pltpu.get_barrier_semaphore()
    greeted = [(wrap(blk + step, nb), col) for step in range(1, nb)] + [up, down]
    greeted += [(blk, y * nx + wrap(x + step, nx)) for step in range(1, nx)]
    for device in greeted:
        pl.semaphore_signal(barrier, inc=1, device_id=device, device_id_type=MESH)
    load_occ.wait()
    turned = occ_in[...].T
    occ_low[blk] = turned[:BS // 2]
    occ_high[blk] = turned[BS // 2:]
    pl.semaphore_wait(barrier, len(greeted))

    def send(src, dst, send_sem, recv_sem, to):
        copy = pltpu.make_async_remote_copy(
            src_ref=src, dst_ref=dst, send_sem=send_sem, recv_sem=recv_sem, device_id=to, device_id_type=MESH
        )
        copy.start()

    def arrive(ref, send_sem, recv_sem, source):
        pltpu.make_async_remote_copy(
            src_ref=ref, dst_ref=ref, send_sem=send_sem, recv_sem=recv_sem, device_id=source, device_id_type=MESH
        ).wait_recv()

    occ = (occ_low, occ_high)

    def occ_view(half, way, step, which=None):
        return occ[half].at[at_z(-step if way == 0 else step, which)]

    def occ_forward(half, way, step):
        for reach in range(half_z, step, -1):
            if OCC_FROM[reach] == step and (reach < half_z or way == half):
                view = occ_view(half, way, step)
                hops = reach - step
                send(view, view, o_send.at[half], o_recv.at[half, way, reach], (at_z(hops if way == 0 else -hops), col))

    def occ_pair(half, way, step):
        view = occ_view(half, way, step)
        send(view, view, op_send.at[half], op_recv.at[half, way, step], pair)

    def occ_steps(half, first, last):
        for step in range(first, min(last, half_z) + 1):
            ways = [way for way in (0, 1) if step < half_z or way == half]
            for way in ways:
                hops = step - OCC_FROM[step]
                arrive(occ_view(half, way, step), o_send.at[half], o_recv.at[half, way, step],
                       (at_z(-hops if way == 0 else hops), col))
                occ_forward(half, way, step)
            for way in ways:
                occ_pair(half, way, step)

    def occ_pair_arrive(half, way, step):
        arrive(occ_view(half, way, step, 1 - core), op_send.at[half], op_recv.at[half, way, step], pair)

    def occ_whole(half):
        occ_pair_arrive(half, 0, 0)
        for step in range(1, half_z + 1):
            for way in (0, 1):
                if step < half_z or way == half:
                    occ_pair_arrive(half, way, step)

    for half in (0, 1):
        occ_forward(half, 0, 0)
        occ_forward(half, 1, 0)
        occ_pair(half, 0, 0)

    def virt_part(part):
        return virt_all.at[y, x, part]

    def virt_source(to):
        return virt_hbm.at[pl.ds(y * share, share), pl.ds(pl.multiple_of(to * BS, BS), BS)]

    def virt_remote(part):
        to = wrap(blk + x + nx * part, nb)
        return pltpu.make_async_remote_copy(
            src_ref=virt_source(to), dst_ref=virt_part(part), send_sem=vz_send.at[part], recv_sem=vz_recv.at[part],
            device_id=(to, col), device_id_type=MESH,
        )

    def virt_local():
        return pltpu.make_async_copy(virt_source(blk), virt_part(0), vz_recv.at[0])

    def virt_start():
        @pl.when(x != 0)
        def _():
            virt_remote(0).start()

        @pl.when(x == 0)
        def _():
            virt_local().start()

        for part in range(1, n_part):
            virt_remote(part).start()

    virt_start()
    load_blocks.wait()

    def order_blocks(index):
        base = index * AUX * BS
        wide[pl.ds(base, AUX * BS), :] = blocks_in[pl.ds(base, AUX * BS), :].astype(jnp.float32)
        for aux in range(AUX):
            blocks[pl.ds(index * BS, BS), pl.ds(aux * BS, BS)] = wide[pl.ds(base + aux, BS, stride=AUX), :].astype(
                jnp.bfloat16
            )

    def virt_arrived():
        @pl.when(x != 0)
        def _():
            virt_remote(0).wait()

        @pl.when(x == 0)
        def _():
            virt_local().wait()

        for part in range(1, n_part):
            virt_remote(part).wait()
        for step in range(1, nx):
            send(virt_all.at[y, x], virt_all.at[y, x], vx_send.at[0], vx_recv.at[step],
                 (blk, y * nx + wrap(x + step, nx)))

    def virt_y_view(way, step, sub):
        return virt_all.at[wrap(y - step if way == 0 else y + step, ny), pl.ds(sub * (nx // 2), nx // 2)]

    def virt_y_send(way, step, sub):
        if step + 1 < half_y or sub == way:
            view = virt_y_view(way, step, sub)
            send(view, view, vy_send.at[0], vy_recv.at[way, step + 1, sub], up if way == 0 else down)

    def virt_y_step(step):
        for sub in (0, 1):
            for way in (0, 1):
                if step < half_y or sub == way:
                    arrive(virt_y_view(way, step, sub), vy_send.at[0], vy_recv.at[way, step, sub],
                           down if way == 0 else up)
                    if step < half_y:
                        virt_y_send(way, step, sub)

    def virt_x_arrived():
        for step in range(1, nx):
            source = wrap(x - step, nx)
            arrive(virt_all.at[y, source], vx_send.at[0], vx_recv.at[step], (blk, y * nx + source))
        for sub in (0, 1):
            virt_y_send(0, 0, sub)
            virt_y_send(1, 0, sub)

    for index in range(n_stored):
        order_blocks(index)
    for first, last in ((1, 3), (4, 6)):
        for half in (0, 1):
            occ_steps(half, first, last)

    sign = 1 - 2 * core
    onward, behind = (at_z(sign), col), (at_z(-sign), col)
    order = [lax.rem(2 * core + turn, AUX) for turn in range(AUX)]

    def s_onward(base, which, step, sub):
        view = s_all.at[base * CORES + which, sub]
        send(view, view, s_send.at[0], s_recv.at[step, which, sub], onward)

    def s_pair(base, which, step, sub):
        view = s_all.at[base * CORES + which, sub]
        send(view, view, sp_send.at[0], sp_recv.at[step, lax.div(sub, 2)], pair)

    def s_pair_arrive(base, step, half):
        arrive(s_all.at[pl.ds(base * CORES, CORES), pl.ds(2 * half, 2)], sp_send.at[0], sp_recv.at[step, half], pair)

    def s_step(step):
        base = wrap(z - sign * step, nz)
        for which in (core, 1 - core):
            for turn, sub in enumerate(order if step + 1 >= half_z else range(AUX)):
                if step < half_z or turn < 2:
                    view = s_all.at[base * CORES + which, sub]
                    arrive(view, s_send.at[0], s_recv.at[step, which, sub], behind)
                    if step + 1 < half_z or (step + 1 == half_z and turn < 2):
                        s_onward(base, which, step + 1, sub)
                    s_pair(base, which, step, sub)

    def s_first(half):
        occ_rows = jnp.concatenate([occ[half][rows_ref[index]] for index in range(n_stored)], axis=1)
        sums = jnp.dot(occ_rows, blocks[...], preferred_element_type=jnp.float32).astype(jnp.bfloat16)
        for aux in range(AUX):
            s_all[blk, 2 * half + aux // 2, aux % 2] = sums[:, aux * BS:(aux + 1) * BS]
        for sub in (2 * half, 2 * half + 1):
            s_onward(z, core, 1, sub)
            view = s_all.at[blk, sub]
            send(view, view, sp_send.at[0], so_recv.at[sub], pair)

    def s_first_pair(half):
        for sub in (2 * half, 2 * half + 1):
            arrive(s_all.at[z * CORES + 1 - core, sub], sp_send.at[0], so_recv.at[sub], pair)
            s_onward(z, 1 - core, 1, sub)

    virt_arrived()
    occ_steps(0, 7, half_z)
    occ_whole(0)
    s_first(0)
    virt_x_arrived()
    occ_steps(1, 7, half_z)
    s_first_pair(0)
    occ_whole(1)
    s_first(1)
    s_first_pair(1)
    picked = jnp.zeros((BS, AUX * BS), jnp.float32)
    for index in range(n_stored):
        here = (rows_ref[index] == col).astype(jnp.float32)
        picked = picked + blocks[index * BS:(index + 1) * BS, :].astype(jnp.float32) * here
    chosen[...] = picked

    def contribute(base, half=None, first=False):
        pieces, rows = [], []
        for which in range(CORES):
            index = base * CORES + which
            if half is None:
                pieces.append(s_all[index].reshape(AUX * BS, BS))
            else:
                pieces.append(s_all[index, pl.ds(2 * half, 2)].reshape(2 * BS, BS))
            away = wrap(blk - index, nb)
            rows.append(virt_all[:, lax.rem(away, nx), lax.div(away, nx)].reshape(BS, BS))
        term = jnp.dot(
            jnp.concatenate(pieces, axis=1), jnp.concatenate(rows, axis=0), preferred_element_type=jnp.float32
        )
        where = slice(None) if half is None else pl.ds(pl.multiple_of(half * 2 * BS, 2 * BS), 2 * BS)
        acc[where, :] = term if first else acc[where, :] + term

    def contribute_step(step):
        mine, other = wrap(z - sign * step, nz), wrap(z + sign * step, nz)
        if step == half_z:
            contribute(mine, core)
            s_pair_arrive(other, step, 1 - core)
            contribute(other, 1 - core)
            return
        contribute(mine, first=step == 0)
        if step > 0:
            for half in (0, 1):
                s_pair_arrive(other, step, half)
            contribute(other)

    virt_steps = [functools.partial(virt_y_step, step) for step in range(1, half_y + 1)]
    done = 0
    for step in range(1, half_z + 1):
        s_step(step)
        if step in VIRT_AT and virt_steps:
            virt_steps.pop(0)()
        if not virt_steps and VIRT_AT[-1] < step < half_z:
            for _ in range(4):
                contribute_step(done)
                done += 1
    for virt_step in virt_steps:
        virt_step()
    while done <= half_z:
        contribute_step(done)
        done += 1

    held = acc[...].astype(jnp.bfloat16).astype(jnp.float32)
    span = BS // 2
    tiles = [
        jnp.concatenate([held[(half * AUX + aux) * span:(half * AUX + aux + 1) * span] for half in (0, 1)], axis=0)
        for aux in range(AUX)
    ]
    sums = []
    for first in range(AUX):
        tile = tiles[first]
        for second in range(AUX):
            sums.append(jnp.sum(tile * chosen[:, second * BS:(second + 1) * BS], axis=0, keepdims=True))
    total = jnp.sum(jnp.concatenate(sums, axis=0), axis=1, keepdims=True)
    pairs = lax.broadcasted_iota(jnp.int32, (AUX * AUX, BS), 0)
    lanes = lax.broadcasted_iota(jnp.int32, (AUX * AUX, BS), 1)
    message = jnp.sum(jnp.where(pairs == lanes, total, 0.0), axis=0, keepdims=True)

    def exchange(buffer, mine, members, stage, device_of, value):
        buffer[mine] = value

        def copy_to(slot, to):
            return pltpu.make_async_remote_copy(
                src_ref=buffer.at[slot], dst_ref=buffer.at[slot], send_sem=r_send.at[stage],
                recv_sem=r_recv.at[stage], device_id=device_of(to), device_id_type=MESH,
            )

        @pl.loop(0, members - 1)
        def _(turn):
            away = lax.div(turn + 1, 2)
            step = members // 2 + away * (1 - 2 * lax.rem(turn, 2))
            copy_to(mine, wrap(mine + step, members)).start()

        def everything():
            some = buffer.at[pl.ds(0, members - 1)]
            return pltpu.make_async_remote_copy(
                src_ref=some, dst_ref=some, send_sem=r_send.at[stage], recv_sem=r_recv.at[stage],
                device_id=device_of(mine), device_id_type=MESH,
            )

        return everything

    over_z = exchange(sum_z, blk, nb, 0, lambda to: (to, col), message)

    for aux in range(AUX):
        spread[pl.ds(aux, BS, stride=AUX), :] = tiles[aux]
    out_ref[...] = spread[...].T.astype(jnp.bfloat16)

    def all_sent(ref, sem, index=0):
        pltpu.make_async_remote_copy(
            src_ref=ref, dst_ref=ref, send_sem=sem.at[index], recv_sem=o_recv.at[0, 0, 0], device_id=pair, device_id_type=MESH
        ).wait_send()

    for half in (0, 1):
        all_sent(occ[half].at[pl.ds(0, nz - 1)], o_send, half)
        all_sent(occ[half].at[pl.ds(0, nz)], op_send, half)
    all_sent(s_all.at[pl.ds(0, nz - 1)], s_send)
    all_sent(s_all.at[pl.ds(0, nz)], sp_send)
    all_sent(virt_all.at[0, pl.ds(0, nx - 1)], vx_send)
    all_sent(virt_all.at[pl.ds(0, ny - 1)], vy_send)

    over_z().wait_recv()
    message = jnp.sum(sum_z[...], axis=0)
    over_col = exchange(sum_c, col, ny * nx, 1, lambda to: (blk, to), message)
    over_z().wait_send()
    over_col().wait_recv()
    message = jnp.sum(sum_c[...], axis=0)

    scale = 1.0 / (BS * math.sqrt(nb * n_stored))
    value = jnp.broadcast_to(message, (AUX, BS)) * scale
    lanes = lax.broadcasted_iota(jnp.int32, (AUX, BS), 1)
    firsts = lax.broadcasted_iota(jnp.int32, (AUX, BS), 0)
    place = lax.broadcasted_iota(jnp.int32, (AUX, AUX), 1)
    response = jnp.zeros((AUX, AUX), jnp.float32)
    for second in range(AUX):
        picked = jnp.sum(jnp.where(lanes == firsts * AUX + second, value, 0.0), axis=1, keepdims=True)
        response = response + jnp.where(place == second, picked, 0.0)
    resp_ref[...] = response
    over_col().wait_send()


def per_device(dims, three_center, block_rows, occupied, virtual):
    nz, ny, nx = dims
    nb = CORES * nz
    n_stored = three_center.shape[0]
    half_z, half_y = nz // 2, ny // 2
    in_hbm = pl.BlockSpec(memory_space=pl.ANY)
    vmem = pl.BlockSpec(memory_space=pltpu.VMEM)
    bf16, f32 = jnp.bfloat16, jnp.float32
    dma = pltpu.SemaphoreType.DMA
    return pl.pallas_call(
        functools.partial(kernel, dims),
        out_shape=(
            jax.ShapeDtypeStruct((BS, AUX * BS), bf16),
            jax.ShapeDtypeStruct((AUX, AUX), f32),
        ),
        in_specs=[pl.BlockSpec(memory_space=pltpu.SMEM), in_hbm, in_hbm, in_hbm],
        out_specs=(vmem, vmem),
        scratch_shapes=[
            pltpu.VMEM((BS, BS), bf16),
            pltpu.VMEM((n_stored * BS * AUX, BS), bf16),
            pltpu.VMEM((n_stored * BS * AUX, BS), f32),
            pltpu.VMEM((n_stored * BS, AUX * BS), bf16),
            pltpu.VMEM((BS, AUX * BS), f32),
            pltpu.VMEM((nb, BS // 2, BS), bf16),
            pltpu.VMEM((nb, BS // 2, BS), bf16),
            pltpu.VMEM((nb, AUX, 2, BS // 2, BS), bf16),
            pltpu.VMEM((ny, nx, nb // nx, BS // ny, BS), bf16),
            pltpu.VMEM((AUX * BS, BS), f32),
            pltpu.VMEM((AUX * BS, BS), f32),
            pltpu.VMEM((nb, 1, BS), f32),
            pltpu.VMEM((ny * nx, 1, BS), f32),
            dma((2,)),
            dma((2,)), dma((2, 2, half_z + 1)),
            dma((2,)), dma((2, 2, half_z + 1)),
            dma((1,)), dma((half_z + 1, CORES, AUX)),
            dma((1,)), dma((half_z + 1, 2)), dma((AUX,)),
            dma((nb // nx,)), dma((nb // nx,)),
            dma((1,)), dma((nx,)),
            dma((1,)), dma((2, half_y + 1, 2)),
            dma((2,)), dma((2,)),
        ],
        compiler_params=pltpu.CompilerParams(
            collective_id=0, has_side_effects=True, vmem_limit_bytes=60 * 1024 * 1024
        ),
    )(block_rows, three_center.reshape(-1, BS), occupied, virtual)


def solution(mesh):
    in_specs = (P("blk", None, None, None), P("blk"), P("blk", "col"), P("blk", None))
    out_specs = (P("blk", "col"), P())
    return jax.shard_map(
        functools.partial(per_device, DIMS), mesh=mesh, in_specs=in_specs, out_specs=out_specs, check_vma=False
    )
```

```python
import functools
import math

import jax
import jax.numpy as jnp
from jax import lax
from jax.experimental import pallas as pl
from jax.experimental.pallas import tpu as pltpu
from jax.sharding import PartitionSpec as P

BS = 128
AUX = 4
CORES = 2
DIMS = (16, 8, 4)
MESH = pl.DeviceIdType.MESH
VIRT_AT = (1, 3, 5, 6)
OCC_FROM = {1: 0, 2: 0, 3: 0, 4: 3, 5: 3, 6: 3, 7: 6, 8: 6}


def kernel(
    dims, rows_ref, blocks_hbm, occ_hbm, virt_hbm, out_ref, resp_ref,
    occ_in, blocks_in, wide, blocks, chosen, occ_low, occ_high, s_all, virt_all, acc, spread, sum_z, sum_c,
    in_sem, o_send, o_recv, op_send, op_recv, s_send, s_recv, sp_send, sp_recv, so_recv,
    vz_send, vz_recv, vx_send, vx_recv, vy_send, vy_recv, r_send, r_recv,
):
    nz, ny, nx = dims
    nb = CORES * nz
    n_stored = blocks.shape[0] // BS
    share = BS // ny
    n_part = nb // nx
    half_z, half_y = nz // 2, ny // 2

    blk, col = lax.axis_index("blk"), lax.axis_index("col")
    z, core = lax.div(blk, CORES), lax.rem(blk, CORES)
    y, x = lax.div(col, nx), lax.rem(col, nx)

    def wrap(value, size):
        return lax.rem(value + 2 * size, size)

    def at_z(step, which=None):
        which = core if which is None else which
        return wrap(z + step, nz) * CORES + which

    right, left = (at_z(1), col), (at_z(-1), col)
    pair = (z * CORES + 1 - core, col)
    up, down = (blk, wrap(y + 1, ny) * nx + x), (blk, wrap(y - 1, ny) * nx + x)

    load_occ = pltpu.make_async_copy(occ_hbm, occ_in, in_sem.at[0])
    load_blocks = pltpu.make_async_copy(blocks_hbm, blocks_in, in_sem.at[1])
    load_occ.start()
    load_blocks.start()

    barrier = pltpu.get_barrier_semaphore()
    greeted = [(wrap(blk + step, nb), col) for step in range(1, nb)] + [up, down]
    greeted += [(blk, y * nx + wrap(x + step, nx)) for step in range(1, nx)]
    for device in greeted:
        pl.semaphore_signal(barrier, inc=1, device_id=device, device_id_type=MESH)
    load_occ.wait()
    turned = occ_in[...].T
    occ_low[blk] = turned[:BS // 2]
    occ_high[blk] = turned[BS // 2:]
    pl.semaphore_wait(barrier, len(greeted))

    def send(src, dst, send_sem, recv_sem, to):
        copy = pltpu.make_async_remote_copy(
            src_ref=src, dst_ref=dst, send_sem=send_sem, recv_sem=recv_sem, device_id=to, device_id_type=MESH
        )
        copy.start()

    def arrive(ref, send_sem, recv_sem, source):
        pltpu.make_async_remote_copy(
            src_ref=ref, dst_ref=ref, send_sem=send_sem, recv_sem=recv_sem, device_id=source, device_id_type=MESH
        ).wait_recv()

    occ = (occ_low, occ_high)

    def occ_view(half, way, step, which=None):
        return occ[half].at[at_z(-step if way == 0 else step, which)]

    def occ_forward(half, way, step):
        for reach in range(half_z, step, -1):
            if OCC_FROM[reach] == step and (reach < half_z or way == half):
                view = occ_view(half, way, step)
                hops = reach - step
                send(view, view, o_send.at[half], o_recv.at[half, way, reach], (at_z(hops if way == 0 else -hops), col))

    def occ_pair(half, way, step):
        view = occ_view(half, way, step)
        send(view, view, op_send.at[half], op_recv.at[half, way, step], pair)

    def occ_steps(half, first, last):
        for step in range(first, min(last, half_z) + 1):
            ways = [way for way in (0, 1) if step < half_z or way == half]
            for way in ways:
                hops = step - OCC_FROM[step]
                arrive(occ_view(half, way, step), o_send.at[half], o_recv.at[half, way, step],
                       (at_z(-hops if way == 0 else hops), col))
                occ_forward(half, way, step)
            for way in ways:
                occ_pair(half, way, step)

    def occ_pair_arrive(half, way, step):
        arrive(occ_view(half, way, step, 1 - core), op_send.at[half], op_recv.at[half, way, step], pair)

    def occ_whole(half):
        occ_pair_arrive(half, 0, 0)
        for step in range(1, half_z + 1):
            for way in (0, 1):
                if step < half_z or way == half:
                    occ_pair_arrive(half, way, step)

    for half in (0, 1):
        occ_forward(half, 0, 0)
        occ_forward(half, 1, 0)
        occ_pair(half, 0, 0)

    def virt_part(part):
        return virt_all.at[y, x, part]

    def virt_source(to):
        return virt_hbm.at[pl.ds(y * share, share), pl.ds(pl.multiple_of(to * BS, BS), BS)]

    def virt_remote(part):
        to = wrap(blk + x + nx * part, nb)
        return pltpu.make_async_remote_copy(
            src_ref=virt_source(to), dst_ref=virt_part(part), send_sem=vz_send.at[part], recv_sem=vz_recv.at[part],
            device_id=(to, col), device_id_type=MESH,
        )

    def virt_local():
        return pltpu.make_async_copy(virt_source(blk), virt_part(0), vz_recv.at[0])

    def virt_start():
        @pl.when(x != 0)
        def _():
            virt_remote(0).start()

        @pl.when(x == 0)
        def _():
            virt_local().start()

        for part in range(1, n_part):
            virt_remote(part).start()

    virt_start()
    load_blocks.wait()

    def order_blocks(index):
        base = index * AUX * BS
        wide[pl.ds(base, AUX * BS), :] = blocks_in[pl.ds(base, AUX * BS), :].astype(jnp.float32)
        for aux in range(AUX):
            blocks[pl.ds(index * BS, BS), pl.ds(aux * BS, BS)] = wide[pl.ds(base + aux, BS, stride=AUX), :].astype(
                jnp.bfloat16
            )

    def virt_arrived():
        @pl.when(x != 0)
        def _():
            virt_remote(0).wait()

        @pl.when(x == 0)
        def _():
            virt_local().wait()

        for part in range(1, n_part):
            virt_remote(part).wait()
        for step in range(1, nx):
            send(virt_all.at[y, x], virt_all.at[y, x], vx_send.at[0], vx_recv.at[step],
                 (blk, y * nx + wrap(x + step, nx)))

    def virt_y_view(way, step, sub):
        return virt_all.at[wrap(y - step if way == 0 else y + step, ny), pl.ds(sub * (nx // 2), nx // 2)]

    def virt_y_send(way, step, sub):
        if step + 1 < half_y or sub == way:
            view = virt_y_view(way, step, sub)
            send(view, view, vy_send.at[0], vy_recv.at[way, step + 1, sub], up if way == 0 else down)

    def virt_y_step(step):
        for sub in (0, 1):
            for way in (0, 1):
                if step < half_y or sub == way:
                    arrive(virt_y_view(way, step, sub), vy_send.at[0], vy_recv.at[way, step, sub],
                           down if way == 0 else up)
                    if step < half_y:
                        virt_y_send(way, step, sub)

    def virt_x_arrived():
        for step in range(1, nx):
            source = wrap(x - step, nx)
            arrive(virt_all.at[y, source], vx_send.at[0], vx_recv.at[step], (blk, y * nx + source))
        for sub in (0, 1):
            virt_y_send(0, 0, sub)
            virt_y_send(1, 0, sub)

    for index in range(n_stored):
        order_blocks(index)
    for first, last in ((1, 3), (4, 6)):
        for half in (0, 1):
            occ_steps(half, first, last)

    sign = 1 - 2 * core
    onward, behind = (at_z(sign), col), (at_z(-sign), col)
    order = [lax.rem(2 * core + turn, AUX) for turn in range(AUX)]

    def s_onward(base, which, step, sub):
        view = s_all.at[base * CORES + which, sub]
        send(view, view, s_send.at[0], s_recv.at[step, which, sub], onward)

    def s_pair(base, which, step, half):
        view = s_all.at[base * CORES + which, pl.ds(2 * half, 2)]
        send(view, view, sp_send.at[0], sp_recv.at[step, half], pair)

    def s_pair_arrive(base, step, half):
        arrive(s_all.at[pl.ds(base * CORES, CORES), pl.ds(2 * half, 2)], sp_send.at[0], sp_recv.at[step, half], pair)

    def s_step(step):
        base = wrap(z - sign * step, nz)
        for which in (core, 1 - core):
            for turn, sub in enumerate(order if step + 1 >= half_z else range(AUX)):
                if step < half_z or turn < 2:
                    view = s_all.at[base * CORES + which, sub]
                    arrive(view, s_send.at[0], s_recv.at[step, which, sub], behind)
                    if step + 1 < half_z or (step + 1 == half_z and turn < 2):
                        s_onward(base, which, step + 1, sub)
                    if turn % 2 == 1:
                        s_pair(base, which, step, lax.div(sub, 2))

    def s_first(half):
        occ_rows = jnp.concatenate([occ[half][rows_ref[index]] for index in range(n_stored)], axis=1)
        sums = jnp.dot(occ_rows, blocks[...], preferred_element_type=jnp.float32).astype(jnp.bfloat16)
        for aux in range(AUX):
            s_all[blk, 2 * half + aux // 2, aux % 2] = sums[:, aux * BS:(aux + 1) * BS]
        for sub in (2 * half, 2 * half + 1):
            s_onward(z, core, 1, sub)
            view = s_all.at[blk, sub]
            send(view, view, sp_send.at[0], so_recv.at[sub], pair)

    def s_first_pair(half):
        for sub in (2 * half, 2 * half + 1):
            arrive(s_all.at[z * CORES + 1 - core, sub], sp_send.at[0], so_recv.at[sub], pair)
            s_onward(z, 1 - core, 1, sub)

    virt_arrived()
    occ_steps(0, 7, half_z)
    occ_whole(0)
    s_first(0)
    virt_x_arrived()
    occ_steps(1, 7, half_z)
    s_first_pair(0)
    occ_whole(1)
    s_first(1)
    s_first_pair(1)
    picked = jnp.zeros((BS, AUX * BS), jnp.float32)
    for index in range(n_stored):
        here = (rows_ref[index] == col).astype(jnp.float32)
        picked = picked + blocks[index * BS:(index + 1) * BS, :].astype(jnp.float32) * here
    chosen[...] = picked

    def contribute(base, half=None, first=False):
        pieces, rows = [], []
        for which in range(CORES):
            index = base * CORES + which
            if half is None:
                pieces.append(s_all[index].reshape(AUX * BS, BS))
            else:
                pieces.append(s_all[index, pl.ds(2 * half, 2)].reshape(2 * BS, BS))
            away = wrap(blk - index, nb)
            rows.append(virt_all[:, lax.rem(away, nx), lax.div(away, nx)].reshape(BS, BS))
        term = jnp.dot(
            jnp.concatenate(pieces, axis=1), jnp.concatenate(rows, axis=0), preferred_element_type=jnp.float32
        )
        where = slice(None) if half is None else pl.ds(pl.multiple_of(half * 2 * BS, 2 * BS), 2 * BS)
        acc[where, :] = term if first else acc[where, :] + term

    def contribute_step(step):
        mine, other = wrap(z - sign * step, nz), wrap(z + sign * step, nz)
        if step == half_z:
            contribute(mine, core)
            s_pair_arrive(other, step, 1 - core)
            contribute(other, 1 - core)
            return
        contribute(mine, first=step == 0)
        if step > 0:
            for half in (0, 1):
                s_pair_arrive(other, step, half)
            contribute(other)

    virt_steps = [functools.partial(virt_y_step, step) for step in range(1, half_y + 1)]
    done = 0
    for step in range(1, half_z + 1):
        s_step(step)
        if step in VIRT_AT and virt_steps:
            virt_steps.pop(0)()
        if not virt_steps and VIRT_AT[-1] < step < half_z:
            for _ in range(4):
                contribute_step(done)
                done += 1
    for virt_step in virt_steps:
        virt_step()
    while done <= half_z:
        contribute_step(done)
        done += 1

    held = acc[...].astype(jnp.bfloat16).astype(jnp.float32)
    span = BS // 2
    tiles = [
        jnp.concatenate([held[(half * AUX + aux) * span:(half * AUX + aux + 1) * span] for half in (0, 1)], axis=0)
        for aux in range(AUX)
    ]
    sums = []
    for first in range(AUX):
        tile = tiles[first]
        for second in range(AUX):
            sums.append(jnp.sum(tile * chosen[:, second * BS:(second + 1) * BS], axis=0, keepdims=True))
    total = jnp.sum(jnp.concatenate(sums, axis=0), axis=1, keepdims=True)
    pairs = lax.broadcasted_iota(jnp.int32, (AUX * AUX, BS), 0)
    lanes = lax.broadcasted_iota(jnp.int32, (AUX * AUX, BS), 1)
    message = jnp.sum(jnp.where(pairs == lanes, total, 0.0), axis=0, keepdims=True)

    def exchange(buffer, mine, members, stage, device_of, value):
        buffer[mine] = value

        def copy_to(slot, to):
            return pltpu.make_async_remote_copy(
                src_ref=buffer.at[slot], dst_ref=buffer.at[slot], send_sem=r_send.at[stage],
                recv_sem=r_recv.at[stage], device_id=device_of(to), device_id_type=MESH,
            )

        @pl.loop(0, members - 1)
        def _(turn):
            away = lax.div(turn + 1, 2)
            step = members // 2 + away * (1 - 2 * lax.rem(turn, 2))
            copy_to(mine, wrap(mine + step, members)).start()

        def everything():
            some = buffer.at[pl.ds(0, members - 1)]
            return pltpu.make_async_remote_copy(
                src_ref=some, dst_ref=some, send_sem=r_send.at[stage], recv_sem=r_recv.at[stage],
                device_id=device_of(mine), device_id_type=MESH,
            )

        return everything

    over_z = exchange(sum_z, blk, nb, 0, lambda to: (to, col), message)

    for aux in range(AUX):
        spread[pl.ds(aux, BS, stride=AUX), :] = tiles[aux]
    out_ref[...] = spread[...].T.astype(jnp.bfloat16)

    def all_sent(ref, sem, index=0):
        pltpu.make_async_remote_copy(
            src_ref=ref, dst_ref=ref, send_sem=sem.at[index], recv_sem=o_recv.at[0, 0, 0], device_id=pair, device_id_type=MESH
        ).wait_send()

    for half in (0, 1):
        all_sent(occ[half].at[pl.ds(0, nz - 1)], o_send, half)
        all_sent(occ[half].at[pl.ds(0, nz)], op_send, half)
    all_sent(s_all.at[pl.ds(0, nz - 1)], s_send)
    all_sent(s_all.at[pl.ds(0, nz)], sp_send)
    all_sent(virt_all.at[0, pl.ds(0, nx - 1)], vx_send)
    all_sent(virt_all.at[pl.ds(0, ny - 1)], vy_send)

    over_z().wait_recv()
    message = jnp.sum(sum_z[...], axis=0)
    over_col = exchange(sum_c, col, ny * nx, 1, lambda to: (blk, to), message)
    over_z().wait_send()
    over_col().wait_recv()
    message = jnp.sum(sum_c[...], axis=0)

    scale = 1.0 / (BS * math.sqrt(nb * n_stored))
    value = jnp.broadcast_to(message, (AUX, BS)) * scale
    lanes = lax.broadcasted_iota(jnp.int32, (AUX, BS), 1)
    firsts = lax.broadcasted_iota(jnp.int32, (AUX, BS), 0)
    place = lax.broadcasted_iota(jnp.int32, (AUX, AUX), 1)
    response = jnp.zeros((AUX, AUX), jnp.float32)
    for second in range(AUX):
        picked = jnp.sum(jnp.where(lanes == firsts * AUX + second, value, 0.0), axis=1, keepdims=True)
        response = response + jnp.where(place == second, picked, 0.0)
    resp_ref[...] = response
    over_col().wait_send()


def per_device(dims, three_center, block_rows, occupied, virtual):
    nz, ny, nx = dims
    nb = CORES * nz
    n_stored = three_center.shape[0]
    half_z, half_y = nz // 2, ny // 2
    in_hbm = pl.BlockSpec(memory_space=pl.ANY)
    vmem = pl.BlockSpec(memory_space=pltpu.VMEM)
    bf16, f32 = jnp.bfloat16, jnp.float32
    dma = pltpu.SemaphoreType.DMA
    return pl.pallas_call(
        functools.partial(kernel, dims),
        out_shape=(
            jax.ShapeDtypeStruct((BS, AUX * BS), bf16),
            jax.ShapeDtypeStruct((AUX, AUX), f32),
        ),
        in_specs=[pl.BlockSpec(memory_space=pltpu.SMEM), in_hbm, in_hbm, in_hbm],
        out_specs=(vmem, vmem),
        scratch_shapes=[
            pltpu.VMEM((BS, BS), bf16),
            pltpu.VMEM((n_stored * BS * AUX, BS), bf16),
            pltpu.VMEM((n_stored * BS * AUX, BS), f32),
            pltpu.VMEM((n_stored * BS, AUX * BS), bf16),
            pltpu.VMEM((BS, AUX * BS), f32),
            pltpu.VMEM((nb, BS // 2, BS), bf16),
            pltpu.VMEM((nb, BS // 2, BS), bf16),
            pltpu.VMEM((nb, AUX, 2, BS // 2, BS), bf16),
            pltpu.VMEM((ny, nx, nb // nx, BS // ny, BS), bf16),
            pltpu.VMEM((AUX * BS, BS), f32),
            pltpu.VMEM((AUX * BS, BS), f32),
            pltpu.VMEM((nb, 1, BS), f32),
            pltpu.VMEM((ny * nx, 1, BS), f32),
            dma((2,)),
            dma((2,)), dma((2, 2, half_z + 1)),
            dma((2,)), dma((2, 2, half_z + 1)),
            dma((1,)), dma((half_z + 1, CORES, AUX)),
            dma((1,)), dma((half_z + 1, 2)), dma((AUX,)),
            dma((nb // nx,)), dma((nb // nx,)),
            dma((1,)), dma((nx,)),
            dma((1,)), dma((2, half_y + 1, 2)),
            dma((2,)), dma((2,)),
        ],
        compiler_params=pltpu.CompilerParams(
            collective_id=0, has_side_effects=True, vmem_limit_bytes=60 * 1024 * 1024
        ),
    )(block_rows, three_center.reshape(-1, BS), occupied, virtual)


def solution(mesh):
    in_specs = (P("blk", None, None, None), P("blk"), P("blk", "col"), P("blk", None))
    out_specs = (P("blk", "col"), P())
    return jax.shard_map(
        functools.partial(per_device, DIMS), mesh=mesh, in_specs=in_specs, out_specs=out_specs, check_vma=False
    )
```
